32 devices in a mesh: replica: 2 (over x), shard: 4 (over z), ctx: 4 (over y, core).
Axes of the slice: x: 2, y: 2, z: 4, core: 2. Of those that a mesh axis runs over, the one named last changes fastest.
Arguments:
- hidden: bfloat16 [4, 1024, 1024], P('replica', ('shard', 'ctx')), may hold values from -6 to 6
- cotangent: bfloat16 [4, 1024, 1024], P('replica', ('shard', 'ctx')), may hold values from -6 to 6
- w_qkv: bfloat16 [1024, 3072], P(('shard', 'ctx')), may hold values from -0.25 to 0.25
- w_out: bfloat16 [1024, 1024], P(('shard', 'ctx')), may hold values from -0.75 to 0.75
- w_in: bfloat16 [1024, 5248], P(('shard', 'ctx')), may hold values from -0.1875 to 0.1875
- w_down: bfloat16 [2624, 1024], P(None, ('shard', 'ctx')), may hold values from -0.25 to 0.25
- norm_attn: bfloat16 [1024], P(('shard', 'ctx')), may hold values from 0.099609375 to 1.8984375
- norm_ffn: bfloat16 [1024], P(('shard', 'ctx')), may hold values from 0.099609375 to 1.8984375
Outputs:
- block_out: bfloat16 [4, 1024, 1024], P('replica', ('shard', 'ctx'))
- grad_hidden: bfloat16 [4, 1024, 1024], P('replica', ('shard', 'ctx'))
- grad_qkv: float32 [1024, 3072], P(('shard', 'ctx'))
- grad_out_proj: float32 [1024, 1024], P(('shard', 'ctx'))
- grad_in_proj: float32 [1024, 5248], P(('shard', 'ctx'))
- grad_down_proj: float32 [2624, 1024], P(None, ('shard', 'ctx'))
- grad_norm_attn: float32 [1024], P(('shard', 'ctx'))
- grad_norm_ffn: float32 [1024], P(('shard', 'ctx'))
The draws below stay inside these ranges and needn't reach their ends.
All inputs are finite; a program needn't handle non-finite values.
Results may differ from the reference program's by a relative error of at most 0.025.
Values may be sent and summed in bfloat16 or wider, within the bound.
A program may use at most 192 MiB of HBM per device.

```python
import jax
import jax.numpy as jnp
from jax import lax

D = 1024
HEADS = 16
HEAD_DIM = 64
FF = 2624
SEQ_LEN = 1024
BATCH = 4


def block_levels(own_key, extent, shards, smallest, high):
    def one(dim, shards_of):
        heights = jax.random.uniform(jax.random.fold_in(jax.random.fold_in(own_key, 6), dim), (shards_of,), jnp.float32, smallest / len(shards), high / len(shards))
        return jnp.repeat(jnp.exp(heights), extent[dim] // shards_of).reshape((-1,) + (1,) * (len(extent) - dim - 1))

    level = one(*shards[0])
    for cut in shards[1:]:
        level = level * one(*cut)
    return level


def bell_draw(key, dims, scale, reach, pieces=(), dtype=jnp.bfloat16):
    entries = scale * jax.random.normal(key, dims, jnp.float32)
    if pieces:
        entries = entries * block_levels(key, dims, pieces, -0.22, 0.18)
    return jnp.clip(entries, -reach, reach).astype(dtype)


def setup_inputs(seed: int = 0) -> dict:
    arg_keys = jax.random.split(jax.random.key(seed), 9)
    return {
        "hidden": bell_draw(arg_keys[0], (BATCH, SEQ_LEN, D), 1.0, 6.0, ((0, 2), (1, 16))),
        "cotangent": bell_draw(arg_keys[1], (BATCH, SEQ_LEN, D), 1.0, 6.0, ((0, 2), (1, 16))),
        "w_qkv": bell_draw(arg_keys[2], (D, 3 * D), (D // 2) ** -0.5, 0.25, ((0, 16),)),
        "w_out": bell_draw(arg_keys[3], (D, D), (D // 16) ** -0.5, 0.75, ((0, 16),)),
        "w_in": bell_draw(arg_keys[4], (D, 2 * FF), D ** -0.5, 0.1875, ((0, 16),)),
        "w_down": bell_draw(arg_keys[5], (FF, D), (FF // 4) ** -0.5, 0.25, ((1, 16),)),
        "norm_attn": jnp.clip(1.0 + 0.18 * jax.random.normal(arg_keys[6], (D,), jnp.float32), 0.099609375, 1.8984375).astype(jnp.bfloat16),
        "norm_ffn": jnp.clip(1.0 + 0.18 * jax.random.normal(arg_keys[7], (D,), jnp.float32), 0.099609375, 1.8984375).astype(jnp.bfloat16),
    }


norm_eps = 1e-05
rope_base = 160000.0
precise = lax.Precision.HIGHEST

@jax.custom_vjp
def low(v):
    return lax.optimization_barrier(v.astype(jnp.bfloat16)).astype(jnp.float32)

@jax.custom_vjp
def low_back(v):
    return v

def low_keep(v):
    return (low(v), None)

def low_pass(kept, grad):
    return (grad,)

def back_keep(v):
    return (v, None)

def back_low(kept, grad):
    return (low(grad),)
low.defvjp(low_keep, low_pass)
low_back.defvjp(back_keep, back_low)

def layer_norm(values, scale_row):
    center = values - lax.optimization_barrier(jnp.mean(values, axis=-1, keepdims=True))
    spread = lax.optimization_barrier(jnp.mean(center * center, axis=-1, keepdims=True))
    return center * lax.rsqrt(spread + norm_eps) * scale_row

def rope_tables(positions):
    frequency = rope_base ** (-jnp.arange(0, HEAD_DIM, 2).astype(jnp.float32) / HEAD_DIM)
    angles = positions.astype(jnp.float32)[:, None] * frequency[None, :]
    angles = jnp.concatenate([angles, angles], axis=-1)
    return (jnp.cos(angles), jnp.sin(angles))

def rotate(values, cos_table, sin_table):
    half_width = values.shape[-1] // 2
    turned = jnp.concatenate([-values[..., half_width:], values[..., :half_width]], axis=-1)
    return values * cos_table + turned * sin_table

def attend(triple):
    queries, keys_rot, values = triple
    scores = low_back(jnp.einsum('qhd,khd->hqk', queries, keys_rot, precision=precise) * HEAD_DIM ** (-0.5))
    weights = jax.nn.softmax(scores, axis=-1)
    return jnp.einsum('hqk,khd->qhd', low(weights), values, precision=precise)

def forward(hidden, w_qkv, w_out, w_in, w_down, norm_attn, norm_ffn):
    flat_in = hidden.reshape(BATCH * SEQ_LEN, D)
    first = low(layer_norm(flat_in, norm_attn))
    packed = low_back(jnp.dot(first, w_qkv, precision=precise)).reshape(BATCH, SEQ_LEN, 3, HEADS, HEAD_DIM)
    cos_table, sin_table = rope_tables(jnp.arange(SEQ_LEN))
    cos_table = cos_table[None, :, None, :]
    sin_table = sin_table[None, :, None, :]
    queries = low(rotate(packed[:, :, 0], cos_table, sin_table))
    keys_rot = low(rotate(packed[:, :, 1], cos_table, sin_table))
    values = low(packed[:, :, 2])
    attended = lax.map(jax.checkpoint(attend), (queries, keys_rot, values))
    attended = low(low_back(attended.reshape(BATCH * SEQ_LEN, D)))
    residual = flat_in + low_back(jnp.dot(attended, w_out, precision=precise))
    second = low(layer_norm(residual, norm_ffn))
    upward = low_back(jnp.dot(second, w_in, precision=precise))
    gated = low(jax.nn.gelu(upward[:, :FF], approximate=False) * upward[:, FF:])
    output = residual + low_back(jnp.dot(gated, w_down, precision=precise))
    return output.reshape(BATCH, SEQ_LEN, D)

def reference(hidden, cotangent, w_qkv, w_out, w_in, w_down, norm_attn, norm_ffn):
    output, pullback = jax.vjp(forward, hidden.astype(jnp.float32), w_qkv.astype(jnp.float32), w_out.astype(jnp.float32), w_in.astype(jnp.float32), w_down.astype(jnp.float32), norm_attn.astype(jnp.float32), norm_ffn.astype(jnp.float32))
    grads = pullback(cotangent.astype(jnp.float32))
    return (output.astype(jnp.bfloat16), grads[0].astype(jnp.bfloat16), grads[1], grads[2], grads[3], grads[4], grads[5], grads[6])
```

```python
import jax
import jax.numpy as jnp
import numpy as np
from jax import lax
from jax.experimental import pallas as pl
from jax.experimental.pallas import tpu as pltpu
from jax.sharding import Mesh, PartitionSpec as P

HEAD_DIM = 64
norm_eps = 1e-05
rope_base = 160000.0
f32 = jnp.float32
bf16 = jnp.bfloat16
CHIPS = ("shard", "cy")
WIDE = 128
BLOCK = 256


def layer_norm(values, scale_row):
    center = values - jnp.mean(values, axis=-1, keepdims=True)
    inverse = lax.rsqrt(jnp.mean(center * center, axis=-1, keepdims=True) + norm_eps)
    normed = center * inverse
    return (normed * scale_row, normed, inverse)


def norm_back(grad_norm, normed, inverse, scale_row):
    scaled = grad_norm * scale_row
    grad_gain = jnp.sum(grad_norm * normed, axis=0)
    grad_input = inverse * (
        scaled
        - jnp.mean(scaled, axis=-1, keepdims=True)
        - normed * jnp.mean(scaled * normed, axis=-1, keepdims=True)
    )
    return (grad_input, grad_gain)


def dot_nn(a, b):
    return lax.dot_general(a, b, (((1,), (0,)), ((), ())), preferred_element_type=f32)


def dot_nt(a, b):
    return lax.dot_general(a, b, (((1,), (1,)), ((), ())), preferred_element_type=f32)


def dot_tn(a, b):
    return lax.dot_general(a, b, (((0,), (0,)), ((), ())), preferred_element_type=f32)


def rope_tables(length):
    frequency = rope_base ** (-np.arange(0, HEAD_DIM, 2, dtype=np.float32) / HEAD_DIM)
    blocks = np.arange(length).reshape(-1, 2, HEAD_DIM)
    orders = np.stack([blocks.reshape(-1), blocks[:, ::-1].reshape(-1)])
    angles = orders.astype(np.float32)[:, :, None] * frequency.astype(np.float32)
    cos = np.tile(np.cos(angles), (1, 1, 4)).astype(np.float32)
    sin = np.sin(angles).astype(np.float32)
    sin = np.concatenate([-sin, sin, -sin, sin], axis=-1)
    return cos, sin


def swap_halves(values):
    lane = lax.broadcasted_iota(jnp.int32, values.shape, 1)
    low = lax.rem(lane, HEAD_DIM) < HEAD_DIM // 2
    return jnp.where(low, pltpu.roll(values, WIDE - 32, 1), pltpu.roll(values, 32, 1))


def head_only(values, head):
    lane = lax.broadcasted_iota(jnp.int32, values.shape, 1)
    inside = (lane < HEAD_DIM) if head == 0 else (lane >= HEAD_DIM)
    return jnp.where(inside, values, jnp.zeros_like(values))


def join_heads(first, second):
    lane = lax.broadcasted_iota(jnp.int32, first.shape, 1)
    return jnp.where(lane < HEAD_DIM, first, second)


def attend_kernel(first, w_qkv, w_out, cos, sin, part, q, k, v, att, lse):
    tokens = first.shape[0]

    @pl.loop(0, tokens // BLOCK)
    def _(i):
        rows = pl.ds(pl.multiple_of(i * BLOCK, BLOCK), BLOCK)
        packed = dot_nn(first[rows, :], w_qkv[...])
        c, s = cos[rows, :], sin[rows, :]
        pq, pk = packed[:, :WIDE], packed[:, WIDE : 2 * WIDE]
        q[rows, :] = (pq * c + swap_halves(pq) * s).astype(bf16)
        k[rows, :] = (pk * c + swap_halves(pk) * s).astype(bf16)
        v[rows, :] = packed[:, 2 * WIDE :].astype(bf16)

    @pl.loop(0, tokens // BLOCK)
    def _(i):
        rows = pl.ds(pl.multiple_of(i * BLOCK, BLOCK), BLOCK)
        q_rows = q[rows, :]
        outs = []
        for head in range(2):
            scores = dot_nt(head_only(q_rows, head), k[...]) * HEAD_DIM**-0.5
            top = jnp.max(scores, axis=-1, keepdims=True)
            exponent = jnp.exp(scores - top)
            total = jnp.sum(exponent, axis=-1, keepdims=True)
            weights = (exponent * (1.0 / total)).astype(bf16)
            outs.append(dot_nn(weights, v[...]))
            lse[rows, head : head + 1] = top + jnp.log(total)
        joined = join_heads(*outs).astype(bf16)
        att[rows, :] = joined
        part[rows, :] = dot_nn(joined, w_out[...]).astype(bf16)


def attend_back_kernel(
    branch, first, w_qkv, w_out, cos, sin, q, k, v, att, lse,
    part, grad_qkv, grad_out, dpacked, dk, dv,
):
    tokens = branch.shape[0]
    dk[...] = jnp.zeros_like(dk)
    dv[...] = jnp.zeros_like(dv)

    @pl.loop(0, tokens // BLOCK)
    def _(i):
        rows = pl.ds(pl.multiple_of(i * BLOCK, BLOCK), BLOCK)
        grad = dot_nt(branch[rows, :], w_out[...]).astype(bf16)
        q_rows = q[rows, :]
        dqs, dks, dvs = [], [], []
        for head in range(2):
            scores = dot_nt(head_only(q_rows, head), k[...]) * HEAD_DIM**-0.5
            probs = jnp.exp(scores - lse[rows, head : head + 1])
            dvs.append(dot_tn(probs.astype(bf16), grad))
            dprobs = dot_nt(head_only(grad, head), v[...])
            dot_sum = jnp.sum(probs * dprobs, axis=-1, keepdims=True)
            dscores = (probs * (dprobs - dot_sum)).astype(bf16)
            dqs.append(dot_nn(dscores, k[...]))
            dks.append(dot_tn(dscores, q_rows))
        dk[...] += join_heads(*dks)
        dv[...] += join_heads(*dvs)
        dq = join_heads(*dqs) * HEAD_DIM**-0.5
        dq = dq * cos[rows, :] - swap_halves(dq) * sin[rows, :]
        dpacked[rows, :WIDE] = dq.astype(bf16)

    @pl.loop(0, tokens // BLOCK)
    def _(i):
        rows = pl.ds(pl.multiple_of(i * BLOCK, BLOCK), BLOCK)
        d = dk[rows, :] * HEAD_DIM**-0.5
        d = d * cos[rows, :] - swap_halves(d) * sin[rows, :]
        dpacked[rows, WIDE : 2 * WIDE] = d.astype(bf16)
        dpacked[rows, 2 * WIDE :] = dv[rows, :].astype(bf16)
        part[rows, :] = dot_nt(dpacked[rows, :], w_qkv[...]).astype(bf16)

    grad_out[...] = dot_tn(att[...], branch[...]).astype(bf16)

    @pl.loop(0, first.shape[1] // BLOCK)
    def _(i):
        cols = pl.ds(pl.multiple_of(i * BLOCK, BLOCK), BLOCK)
        grad_qkv[cols, :] = dot_tn(first[:, cols], dpacked[...]).astype(bf16)


def call(kernel, outs, scratch, *args):
    vmem = pl.BlockSpec(memory_space=pltpu.VMEM)
    return pl.pallas_call(
        kernel,
        out_shape=[jax.ShapeDtypeStruct(s, d) for s, d in outs],
        in_specs=[vmem] * len(args),
        out_specs=[vmem] * len(outs),
        scratch_shapes=[pltpu.VMEM(s, d) for s, d in scratch],
        compiler_params=pltpu.CompilerParams(vmem_limit_bytes=48 * 2**20),
    )(*args)


def gate_mix(upward):
    half_width = upward.shape[1] // 2
    return jax.nn.gelu(upward[:, :half_width], approximate=False) * upward[:, half_width:]


def swap_core(value):
    return lax.ppermute(value, "core", [(0, 1), (1, 0)])


def on_device(replicas, chips, hidden, cotangent, w_qkv, w_out, w_in, w_down, norm_attn, norm_ffn):
    _, local_len, features = hidden.shape
    units = w_down.shape[0] // chips
    core = lax.axis_index("core")
    take = lambda value, axis, index: lax.dynamic_index_in_dim(value, index, axis, keepdims=False)

    gains = lax.all_gather(
        jnp.stack([norm_attn, norm_ffn]), CHIPS + ("core",), axis=1, tiled=True
    ).astype(f32)
    other = swap_core(jnp.stack([take(hidden, 0, 1 - core), take(cotangent, 0, 1 - core)]))
    x = jnp.concatenate([take(hidden, 0, core), other[0]]).astype(f32)
    grad_top = jnp.concatenate([take(cotangent, 0, core), other[1]])

    def spread(blocks):
        moved = lax.all_to_all(blocks, CHIPS, 0, 0, tiled=True)
        both = lax.all_gather(moved, "core", axis=1, tiled=True)
        return both.reshape(features, blocks.shape[-1])

    rows = w_qkv.shape[0]
    qkv_own = spread(
        w_qkv.reshape(rows, 3, chips, WIDE).transpose(2, 0, 1, 3).reshape(chips, rows, 3 * WIDE)
    )
    ffn_own = spread(
        jnp.concatenate(
            [
                w_in.reshape(rows, 2, chips, units).transpose(2, 0, 1, 3).reshape(chips, rows, -1),
                w_down.reshape(chips, units, rows).transpose(0, 2, 1),
            ],
            axis=2,
        )
    )
    in_own, down_own = ffn_own[:, : 2 * units], ffn_own[:, 2 * units :]
    out_own = lax.all_gather(w_out, "core", axis=0, tiled=True)

    def gather(value):
        return lax.all_gather(value, CHIPS, axis=0, tiled=True)

    def scatter(value):
        return lax.psum_scatter(value, CHIPS, scatter_dimension=0, tiled=True).astype(f32)

    normed_one, centered_one, inverse_one = layer_norm(x, gains[0])
    first = gather(normed_one.astype(bf16))
    top_all = gather(grad_top)
    tokens = first.shape[0]
    cos_np, sin_np = rope_tables(tokens)
    cos = take(jnp.asarray(cos_np), 0, core)
    sin = take(jnp.asarray(sin_np), 0, core)
    narrow = ((tokens, WIDE), bf16)
    part, q, k, v, att, lse = call(
        attend_kernel,
        [((tokens, features), bf16), narrow, narrow, narrow, narrow, ((tokens, 2), f32)],
        [],
        first, qkv_own, out_own, cos, sin,
    )
    residual = x + scatter(part)
    normed_two, centered_two, inverse_two = layer_norm(residual, gains[1])
    second = gather(normed_two.astype(bf16))
    upward = dot_nn(second, in_own)
    gated, gate_back = jax.vjp(gate_mix, upward)
    gated = gated.astype(bf16)
    grad_gated = dot_nn(top_all, down_own)
    grad_up = gate_back(grad_gated)[0].astype(bf16)
    grad_second = scatter(dot_nt(grad_up, in_own).astype(bf16))
    block_out = (residual + scatter(dot_nt(gated, down_own).astype(bf16))).astype(bf16)
    grad_norm_two, grad_gain_ffn = norm_back(grad_second, centered_two, inverse_two, gains[1])
    grad_resid = grad_top.astype(f32) + grad_norm_two
    branch = gather(grad_resid.astype(bf16))
    grad_ffn = jnp.concatenate(
        [dot_tn(second, grad_up).astype(bf16), dot_tn(top_all, gated).astype(bf16)], axis=1
    )

    def over_core(value):
        return take(value, 1, core).astype(f32) + swap_core(take(value, 1, 1 - core)).astype(f32)

    def over_replicas(value):
        if replicas == 2:
            return value.astype(f32) + lax.ppermute(value, "replica", [(0, 1), (1, 0)]).astype(f32)
        return lax.psum(value, "replica").astype(f32)

    def collect(value):
        halves = over_core(value.reshape(chips, 2, rows, value.shape[-1])).astype(bf16)
        return lax.all_to_all(halves, CHIPS, 0, 0, tiled=True)

    ffn_sum = over_replicas(collect(grad_ffn))
    grad_in = ffn_sum[:, :, : 2 * units].reshape(chips, rows, 2, units)
    grad_in = grad_in.transpose(1, 2, 0, 3).reshape(w_in.shape)
    grad_down = ffn_sum[:, :, 2 * units :].transpose(0, 2, 1).reshape(w_down.shape)

    part, grad_qkv, grad_out = call(
        attend_back_kernel,
        [((tokens, features), bf16), ((features, 3 * WIDE), bf16), ((WIDE, features), bf16)],
        [((tokens, 3 * WIDE), bf16), ((tokens, WIDE), f32), ((tokens, WIDE), f32)],
        branch, first, qkv_own, out_own, cos, sin, q, k, v, att, lse,
    )
    grad_first = scatter(part)
    grad_norm_one, grad_gain_attn = norm_back(grad_first, centered_one, inverse_one, gains[0])
    grad_hidden = (grad_resid + grad_norm_one).astype(bf16)
    grad_out = over_core(grad_out.reshape(1, 2, rows, features))[0].astype(bf16)
    grad_out = over_replicas(grad_out)

    qkv_sum = over_replicas(collect(grad_qkv))
    grad_qkv = qkv_sum.reshape(chips, rows, 3, WIDE).transpose(1, 2, 0, 3).reshape(w_qkv.shape)
    gain_parts = jnp.stack([grad_gain_attn, grad_gain_ffn])
    gain_sum = lax.psum(gain_parts, ("replica",) + CHIPS + ("core",))
    own = lax.axis_index(CHIPS + ("core",)) * rows
    gain_sum = lax.dynamic_slice_in_dim(gain_sum, own, rows, 1)

    done = jnp.stack([block_out, grad_hidden])
    back = swap_core(done[:, local_len:])
    mine = done[:, :local_len]
    pair = jnp.where(core == 0, jnp.stack([mine, back], 1), jnp.stack([back, mine], 1))
    return (pair[0], pair[1], grad_qkv, grad_out, grad_in, grad_down, gain_sum[0], gain_sum[1])


def solution(mesh):
    replicas, shards, ctx = (mesh.shape[name] for name in ("replica", "shard", "ctx"))
    fine = Mesh(
        mesh.devices.reshape(replicas, shards, ctx // 2, 2), ("replica", "shard", "cy", "core")
    )
    group = ("shard", "cy", "core")
    token = P("replica", group, None)
    row, col, vec = P(group, None), P(None, group), P(group)

    def body(*args):
        return on_device(replicas, shards * ctx // 2, *args)

    return jax.shard_map(
        body,
        mesh=fine,
        in_specs=(token, token, row, row, row, col, vec, vec),
        out_specs=(token, token, row, row, row, col, vec, vec),
        check_vma=False,
    )
```

```python
import jax
import jax.numpy as jnp
import numpy as np
from jax import lax
from jax.experimental import pallas as pl
from jax.experimental.pallas import tpu as pltpu
from jax.sharding import Mesh, PartitionSpec as P

HEAD_DIM = 64
norm_eps = 1e-05
rope_base = 160000.0
f32 = jnp.float32
bf16 = jnp.bfloat16
CHIPS = ("shard", "cy")
WIDE = 128
BLOCK = 256


def layer_norm(values, scale_row):
    center = values - jnp.mean(values, axis=-1, keepdims=True)
    inverse = lax.rsqrt(jnp.mean(center * center, axis=-1, keepdims=True) + norm_eps)
    normed = center * inverse
    return (normed * scale_row, normed, inverse)


def norm_back(grad_norm, normed, inverse, scale_row):
    scaled = grad_norm * scale_row
    grad_gain = jnp.sum(grad_norm * normed, axis=0)
    grad_input = inverse * (
        scaled
        - jnp.mean(scaled, axis=-1, keepdims=True)
        - normed * jnp.mean(scaled * normed, axis=-1, keepdims=True)
    )
    return (grad_input, grad_gain)


def dot_nn(a, b):
    return lax.dot_general(a, b, (((1,), (0,)), ((), ())), preferred_element_type=f32)


def dot_nt(a, b):
    return lax.dot_general(a, b, (((1,), (1,)), ((), ())), preferred_element_type=f32)


def dot_tn(a, b):
    return lax.dot_general(a, b, (((0,), (0,)), ((), ())), preferred_element_type=f32)


def rope_tables(length):
    frequency = rope_base ** (-np.arange(0, HEAD_DIM, 2, dtype=np.float32) / HEAD_DIM)
    blocks = np.arange(length).reshape(-1, 2, HEAD_DIM)
    orders = np.stack([blocks.reshape(-1), blocks[:, ::-1].reshape(-1)])
    angles = orders.astype(np.float32)[:, :, None] * frequency.astype(np.float32)
    cos = np.tile(np.cos(angles), (1, 1, 4)).astype(np.float32)
    sin = np.sin(angles).astype(np.float32)
    sin = np.concatenate([-sin, sin, -sin, sin], axis=-1)
    return cos, sin


def swap_halves(values):
    lane = lax.broadcasted_iota(jnp.int32, values.shape, 1)
    low = lax.rem(lane, HEAD_DIM) < HEAD_DIM // 2
    return jnp.where(low, pltpu.roll(values, WIDE - 32, 1), pltpu.roll(values, 32, 1))


def head_only(values, head):
    lane = lax.broadcasted_iota(jnp.int32, values.shape, 1)
    inside = (lane < HEAD_DIM) if head == 0 else (lane >= HEAD_DIM)
    return jnp.where(inside, values, jnp.zeros_like(values))


def join_heads(first, second):
    lane = lax.broadcasted_iota(jnp.int32, first.shape, 1)
    return jnp.where(lane < HEAD_DIM, first, second)


def attend_kernel(first, w_qkv, w_out, cos, sin, part, q, k, v, att, lse):
    tokens = first.shape[0]

    @pl.loop(0, tokens // BLOCK)
    def _(i):
        rows = pl.ds(pl.multiple_of(i * BLOCK, BLOCK), BLOCK)
        packed = dot_nn(first[rows, :], w_qkv[...])
        c, s = cos[rows, :], sin[rows, :]
        pq, pk = packed[:, :WIDE], packed[:, WIDE : 2 * WIDE]
        q[rows, :] = (pq * c + swap_halves(pq) * s).astype(bf16)
        k[rows, :] = (pk * c + swap_halves(pk) * s).astype(bf16)
        v[rows, :] = packed[:, 2 * WIDE :].astype(bf16)

    @pl.loop(0, tokens // BLOCK)
    def _(i):
        rows = pl.ds(pl.multiple_of(i * BLOCK, BLOCK), BLOCK)
        q_rows = q[rows, :]
        outs = []
        for head in range(2):
            scores = dot_nt(head_only(q_rows, head), k[...]) * HEAD_DIM**-0.5
            top = jnp.max(scores, axis=-1, keepdims=True)
            exponent = jnp.exp(scores - top)
            total = jnp.sum(exponent, axis=-1, keepdims=True)
            weights = (exponent * (1.0 / total)).astype(bf16)
            outs.append(dot_nn(weights, v[...]))
            lse[rows, head : head + 1] = top + jnp.log(total)
        joined = join_heads(*outs).astype(bf16)
        att[rows, :] = joined
        part[rows, :] = dot_nn(joined, w_out[...]).astype(bf16)


def attend_back_kernel(
    branch, first, w_qkv, w_out, cos, sin, q, k, v, att, lse,
    part, grad_qkv, grad_out, dpacked, dk, dv,
):
    tokens = branch.shape[0]
    dk[...] = jnp.zeros_like(dk)
    dv[...] = jnp.zeros_like(dv)

    @pl.loop(0, tokens // BLOCK)
    def _(i):
        rows = pl.ds(pl.multiple_of(i * BLOCK, BLOCK), BLOCK)
        grad = dot_nt(branch[rows, :], w_out[...]).astype(bf16)
        q_rows = q[rows, :]
        dqs, dks, dvs = [], [], []
        for head in range(2):
            scores = dot_nt(head_only(q_rows, head), k[...]) * HEAD_DIM**-0.5
            probs = jnp.exp(scores - lse[rows, head : head + 1])
            dvs.append(dot_tn(probs.astype(bf16), grad))
            dprobs = dot_nt(head_only(grad, head), v[...])
            dot_sum = jnp.sum(probs * dprobs, axis=-1, keepdims=True)
            dscores = (probs * (dprobs - dot_sum)).astype(bf16)
            dqs.append(dot_nn(dscores, k[...]))
            dks.append(dot_tn(dscores, q_rows))
        dk[...] += join_heads(*dks)
        dv[...] += join_heads(*dvs)
        dq = join_heads(*dqs) * HEAD_DIM**-0.5
        dq = dq * cos[rows, :] - swap_halves(dq) * sin[rows, :]
        dpacked[rows, :WIDE] = dq.astype(bf16)

    @pl.loop(0, tokens // BLOCK)
    def _(i):
        rows = pl.ds(pl.multiple_of(i * BLOCK, BLOCK), BLOCK)
        d = dk[rows, :] * HEAD_DIM**-0.5
        d = d * cos[rows, :] - swap_halves(d) * sin[rows, :]
        dpacked[rows, WIDE : 2 * WIDE] = d.astype(bf16)
        dpacked[rows, 2 * WIDE :] = dv[rows, :].astype(bf16)
        part[rows, :] = dot_nt(dpacked[rows, :], w_qkv[...]).astype(bf16)

    grad_out[...] = dot_tn(att[...], branch[...]).astype(bf16)

    @pl.loop(0, first.shape[1] // BLOCK)
    def _(i):
        cols = pl.ds(pl.multiple_of(i * BLOCK, BLOCK), BLOCK)
        grad_qkv[cols, :] = dot_tn(first[:, cols], dpacked[...]).astype(bf16)


def call(kernel, outs, scratch, *args):
    vmem = pl.BlockSpec(memory_space=pltpu.VMEM)
    return pl.pallas_call(
        kernel,
        out_shape=[jax.ShapeDtypeStruct(s, d) for s, d in outs],
        in_specs=[vmem] * len(args),
        out_specs=[vmem] * len(outs),
        scratch_shapes=[pltpu.VMEM(s, d) for s, d in scratch],
        compiler_params=pltpu.CompilerParams(vmem_limit_bytes=48 * 2**20),
    )(*args)


def comm_kernel(shards, kinds, *refs):
    count = len(kinds)
    ins, outs, rest = refs[:count], refs[count : 2 * count], list(refs[2 * count :])
    s, y, c = (lax.axis_index(name) for name in ("shard", "cy", "core"))
    chips = 2 * shards
    me = 2 * s + y
    spreads = "spread" in kinds
    barrier = pltpu.get_barrier_semaphore()
    for step in range(1, chips):
        peer = lax.rem(me + step, chips)
        pl.semaphore_signal(barrier, inc=1, device_id=at_chip(peer // 2, lax.rem(peer, 2)), device_id_type=MESH)
    if spreads:
        pl.semaphore_signal(barrier, inc=1, device_id={"core": 1 - c}, device_id_type=MESH)
    pl.semaphore_wait(barrier, chips if spreads else chips - 1)

    def far(d):
        return lax.rem(s + d, shards)

    stages = [[], [], []]
    for kind, src, dst in zip(kinds, ins, outs):
        send, recv = rest.pop(0), rest.pop(0)
        scratch = [rest.pop(0) for _ in range(2 if kind == "rs" else 0)]
        for stage, step in zip(stages, MOVES[kind](src, dst, send, recv, scratch, shards, s, y, c, far)):
            stage.append(step)
    for stage in stages:
        for step in stage:
            step()


MESH = pl.DeviceIdType.MESH


def at_chip(shard, cy):
    return {"shard": shard, "cy": cy}


def remote(src, dst, send, recv, where):
    return pltpu.make_async_remote_copy(
        src_ref=src, dst_ref=dst, send_sem=send, recv_sem=recv, device_id=where, device_id_type=MESH
    )


def gather_moves(src, dst, send, recv, scratch, shards, s, y, c, far):
    size = src.shape[0]

    def place(shard, cy):
        return dst.at[pl.ds(pl.multiple_of((2 * shard + cy) * size, size), size), :]

    across = remote(src, place(s, y), send.at[0], recv.at[0], at_chip(s, 1 - y))
    along = [
        remote(src, place(s, y), send.at[d], recv.at[d], at_chip(far(d), y))
        for d in range(1, shards)
    ]
    onward = []
    for d in range(1, shards):
        spot = place(far(shards - d), y)
        slot = shards - 1 + d
        onward.append(remote(spot, spot, send.at[slot], recv.at[slot], at_chip(s, 1 - y)))

    def begin():
        for copy in along:
            copy.start()
        across.start()
        place(s, y)[...] = src[...]

    def middle():
        for first, second in zip(along, onward):
            first.wait_recv()
            second.start()

    def finish():
        for copy in along:
            copy.wait_send()
        across.wait()
        for copy in onward:
            copy.wait()

    return begin, middle, finish


def scatter_moves(src, dst, send, recv, scratch, shards, s, y, c, far):
    size = dst.shape[0]
    ybuf, zbuf = scratch

    def part(shard, cy):
        return src.at[pl.ds(pl.multiple_of((2 * shard + cy) * size, size), size), :]

    order = list(range(1, shards)) + [0]
    across = {
        d: remote(part(far(d), 1 - y), ybuf.at[d], send.at[d], recv.at[d], at_chip(s, 1 - y))
        for d in order
    }
    along = {
        d: remote(
            ybuf.at[shards + d], zbuf.at[d], send.at[shards + d], recv.at[shards + d],
            at_chip(far(d), y),
        )
        for d in range(1, shards)
    }

    def begin():
        for d in order:
            across[d].start()

    def middle():
        for d in range(1, shards):
            across[d].wait_recv()
            ybuf[shards + d] = (part(far(d), y)[...].astype(f32) + ybuf[d].astype(f32)).astype(bf16)
            along[d].start()

    def finish():
        across[0].wait_recv()
        total = part(s, y)[...].astype(f32) + ybuf[0].astype(f32)
        for d in range(1, shards):
            along[d].wait_recv()
            total = total + zbuf[d].astype(f32)
        dst[...] = total
        for d in order:
            across[d].wait_send()
        for d in range(1, shards):
            along[d].wait_send()

    return begin, middle, finish


def swap_moves(src, dst, send, recv, scratch, shards, s, y, c, far, share=False):
    chips, size = 2 * shards, src.shape[1]
    me = 2 * s + y

    def place(chip):
        if share:
            return dst.at[chip, pl.ds(pl.multiple_of(c * size, size), size), :]
        return dst.at[chip]

    out, onward = [], []
    for e in range(1, chips):
        peer = lax.rem(me + e, chips)
        out.append(
            remote(
                src.at[peer], place(me), send.at[e], recv.at[e],
                at_chip(peer // 2, lax.rem(peer, 2)),
            )
        )
    for e in range(chips if share else 0):
        spot = place(lax.rem(me + chips - e, chips))
        first = src.at[me] if e == 0 else spot
        onward.append(remote(first, spot, send.at[chips + e], recv.at[chips + e], {"core": 1 - c}))

    def begin():
        for copy in out:
            copy.start()
        if share:
            onward[0].start()
        place(me)[...] = src[me]

    def middle():
        for e in range(1, chips):
            out[e - 1].wait_recv()
            if share:
                onward[e].start()

    def finish():
        for copy in out:
            copy.wait_send()
        for copy in onward:
            copy.wait()

    return begin, middle, finish


def spread_moves(*args):
    return swap_moves(*args, share=True)


MOVES = {"ag": gather_moves, "rs": scatter_moves, "a2a": swap_moves, "spread": spread_moves}


def exchange(shards, ident, *jobs):
    chips = 2 * shards
    outs, scratch = [], []
    for kind, value in jobs:
        shape, dtype = value.shape, value.dtype
        slots = {"ag": chips, "rs": chips, "a2a": chips, "spread": 2 * chips}[kind]
        scratch += [pltpu.SemaphoreType.DMA((slots,))] * 2
        if kind == "ag":
            shape = (chips * shape[0], shape[1])
        elif kind == "rs":
            shape, dtype = (shape[0] // chips, shape[1]), f32
            scratch += [pltpu.VMEM((chips,) + shape, bf16), pltpu.VMEM((shards,) + shape, bf16)]
        elif kind == "spread":
            shape = (shape[0], 2 * shape[1], shape[2])
        outs.append(jax.ShapeDtypeStruct(shape, dtype))
    vmem = pl.BlockSpec(memory_space=pltpu.VMEM)
    kinds = tuple(kind for kind, _ in jobs)
    return pl.pallas_call(
        lambda *refs: comm_kernel(shards, kinds, *refs),
        out_shape=outs,
        in_specs=[vmem] * len(jobs),
        out_specs=[vmem] * len(jobs),
        scratch_shapes=scratch,
        compiler_params=pltpu.CompilerParams(
            collective_id=ident, has_side_effects=True, vmem_limit_bytes=48 * 2**20
        ),
    )(*[value for _, value in jobs])


def gate_mix(upward):
    half_width = upward.shape[1] // 2
    return jax.nn.gelu(upward[:, :half_width], approximate=False) * upward[:, half_width:]


def swap_core(value):
    return lax.ppermute(value, "core", [(0, 1), (1, 0)])


def on_device(replicas, shards, hidden, cotangent, w_qkv, w_out, w_in, w_down, norm_attn, norm_ffn):
    _, local_len, features = hidden.shape
    chips = 2 * shards
    units = w_down.shape[0] // chips
    core = lax.axis_index("core")
    take = lambda value, axis, index: lax.dynamic_index_in_dim(value, index, axis, keepdims=False)

    gain_pair = jnp.concatenate([norm_attn, norm_ffn])
    gain_other = swap_core(gain_pair)
    gain_rows = jnp.where(
        core == 0, jnp.stack([gain_pair, gain_other]), jnp.stack([gain_other, gain_pair])
    )
    (gains,) = exchange(shards, 0, ("ag", jnp.pad(gain_rows, ((0, 14), (0, 0)))))
    gains = gains.reshape(chips, 16, 2, -1)[:, :2].transpose(2, 0, 1, 3).reshape(2, features)
    gains = gains.astype(f32)
    other = swap_core(jnp.stack([take(hidden, 0, 1 - core), take(cotangent, 0, 1 - core)]))
    x = jnp.concatenate([take(hidden, 0, core), other[0]]).astype(f32)
    grad_top = jnp.concatenate([take(cotangent, 0, core), other[1]])

    rows = w_qkv.shape[0]
    qkv_blocks = (
        w_qkv.reshape(rows, 3, chips, WIDE).transpose(2, 0, 1, 3).reshape(chips, rows, 3 * WIDE)
    )
    ffn_blocks = jnp.concatenate(
        [
            w_in.reshape(rows, 2, chips, units).transpose(2, 0, 1, 3).reshape(chips, rows, -1),
            w_down.reshape(chips, units, rows).transpose(0, 2, 1),
        ],
        axis=2,
    )
    out_own = lax.all_gather(w_out, "core", axis=0, tiled=True)

    def gather(value):
        return lax.all_gather(value, CHIPS, axis=0, tiled=True)

    normed_one, centered_one, inverse_one = layer_norm(x, gains[0])
    first, qkv_own = exchange(
        shards, 1, ("ag", normed_one.astype(bf16)), ("spread", qkv_blocks)
    )
    qkv_own = qkv_own.reshape(features, 3 * WIDE)
    top_all = gather(grad_top)
    tokens = first.shape[0]
    cos_np, sin_np = rope_tables(tokens)
    cos = take(jnp.asarray(cos_np), 0, core)
    sin = take(jnp.asarray(sin_np), 0, core)
    narrow = ((tokens, WIDE), bf16)
    part, q, k, v, att, lse = call(
        attend_kernel,
        [((tokens, features), bf16), narrow, narrow, narrow, narrow, ((tokens, 2), f32)],
        [],
        first, qkv_own, out_own, cos, sin,
    )
    attn_sum, ffn_own = exchange(shards, 2, ("rs", part), ("spread", ffn_blocks))
    ffn_own = ffn_own.reshape(features, 3 * units)
    in_own, down_own = ffn_own[:, : 2 * units], ffn_own[:, 2 * units :]
    residual = x + attn_sum
    normed_two, centered_two, inverse_two = layer_norm(residual, gains[1])
    (second,) = exchange(shards, 3, ("ag", normed_two.astype(bf16)))
    upward = dot_nn(second, in_own)
    gated, gate_back = jax.vjp(gate_mix, upward)
    gated = gated.astype(bf16)
    grad_gated = dot_nn(top_all, down_own)
    grad_up = gate_back(grad_gated)[0].astype(bf16)
    grad_second, down_sum = exchange(
        shards,
        4,
        ("rs", dot_nt(grad_up, in_own).astype(bf16)),
        ("rs", dot_nt(gated, down_own).astype(bf16)),
    )
    block_out = (residual + down_sum).astype(bf16)
    grad_norm_two, grad_gain_ffn = norm_back(grad_second, centered_two, inverse_two, gains[1])
    grad_resid = grad_top.astype(f32) + grad_norm_two
    (branch,) = exchange(shards, 5, ("ag", grad_resid.astype(bf16)))
    grad_ffn = jnp.concatenate(
        [dot_tn(second, grad_up).astype(bf16), dot_tn(top_all, gated).astype(bf16)], axis=1
    )

    def over_core(value):
        return take(value, 1, core).astype(f32) + swap_core(take(value, 1, 1 - core)).astype(f32)

    def over_replicas(value):
        if replicas == 2:
            return value.astype(f32) + lax.ppermute(value, "replica", [(0, 1), (1, 0)]).astype(f32)
        return lax.psum(value, "replica").astype(f32)

    def halves(value):
        return over_core(value.reshape(chips, 2, rows, value.shape[-1])).astype(bf16)

    part, grad_qkv, grad_out = call(
        attend_back_kernel,
        [((tokens, features), bf16), ((features, 3 * WIDE), bf16), ((WIDE, features), bf16)],
        [((tokens, 3 * WIDE), bf16), ((tokens, WIDE), f32), ((tokens, WIDE), f32)],
        branch, first, qkv_own, out_own, cos, sin, q, k, v, att, lse,
    )
    grad_first, ffn_sum, qkv_sum = exchange(
        shards, 6, ("rs", part), ("a2a", halves(grad_ffn)), ("a2a", halves(grad_qkv))
    )
    ffn_sum = over_replicas(ffn_sum)
    qkv_sum = over_replicas(qkv_sum)
    grad_in = ffn_sum[:, :, : 2 * units].reshape(chips, rows, 2, units)
    grad_in = grad_in.transpose(1, 2, 0, 3).reshape(w_in.shape)
    grad_down = ffn_sum[:, :, 2 * units :].transpose(0, 2, 1).reshape(w_down.shape)
    grad_norm_one, grad_gain_attn = norm_back(grad_first, centered_one, inverse_one, gains[0])
    grad_hidden = (grad_resid + grad_norm_one).astype(bf16)
    grad_out = over_core(grad_out.reshape(1, 2, rows, features))[0].astype(bf16)
    grad_out = over_replicas(grad_out)

    grad_qkv = qkv_sum.reshape(chips, rows, 3, WIDE).transpose(1, 2, 0, 3).reshape(w_qkv.shape)
    gain_parts = jnp.stack([grad_gain_attn, grad_gain_ffn])
    gain_parts = gain_parts.reshape(2, chips, 2, rows)
    gain_half = take(gain_parts, 2, core) + swap_core(take(gain_parts, 2, 1 - core))
    gain_half = gain_half.transpose(1, 0, 2).reshape(chips, 1, 2 * rows)
    (gain_sum,) = exchange(
        shards, 7, ("a2a", jnp.broadcast_to(gain_half, (chips, 8, 2 * rows)))
    )
    gain_sum = over_replicas(jnp.sum(gain_sum[:, 0], axis=0)).reshape(2, rows)

    done = jnp.stack([block_out, grad_hidden])
    back = swap_core(done[:, local_len:])
    mine = done[:, :local_len]
    pair = jnp.where(core == 0, jnp.stack([mine, back], 1), jnp.stack([back, mine], 1))
    return (pair[0], pair[1], grad_qkv, grad_out, grad_in, grad_down, gain_sum[0], gain_sum[1])


def solution(mesh):
    replicas, shards, ctx = (mesh.shape[name] for name in ("replica", "shard", "ctx"))
    fine = Mesh(
        mesh.devices.reshape(replicas, shards, ctx // 2, 2), ("replica", "shard", "cy", "core")
    )
    group = ("shard", "cy", "core")
    token = P("replica", group, None)
    row, col, vec = P(group, None), P(None, group), P(group)

    def body(*args):
        return on_device(replicas, shards, *args)

    return jax.shard_map(
        body,
        mesh=fine,
        in_specs=(token, token, row, row, row, col, vec, vec),
        out_specs=(token, token, row, row, row, col, vec, vec),
        check_vma=False,
    )
```

```python
import jax
import jax.numpy as jnp
import numpy as np
from jax import lax
from jax.experimental import pallas as pl
from jax.experimental.pallas import tpu as pltpu
from jax.sharding import Mesh, PartitionSpec as P

HEAD_DIM = 64
norm_eps = 1e-05
rope_base = 160000.0
f32 = jnp.float32
bf16 = jnp.bfloat16
CHIPS = ("shard", "cy")
WIDE = 128
BLOCK = 256


def layer_norm(values, scale_row):
    center = values - jnp.mean(values, axis=-1, keepdims=True)
    inverse = lax.rsqrt(jnp.mean(center * center, axis=-1, keepdims=True) + norm_eps)
    normed = center * inverse
    return (normed * scale_row, normed, inverse)


def norm_back(grad_norm, normed, inverse, scale_row):
    scaled = grad_norm * scale_row
    grad_gain = jnp.sum(grad_norm * normed, axis=0)
    grad_input = inverse * (
        scaled
        - jnp.mean(scaled, axis=-1, keepdims=True)
        - normed * jnp.mean(scaled * normed, axis=-1, keepdims=True)
    )
    return (grad_input, grad_gain)


def dot_nn(a, b):
    return lax.dot_general(a, b, (((1,), (0,)), ((), ())), preferred_element_type=f32)


def dot_nt(a, b):
    return lax.dot_general(a, b, (((1,), (1,)), ((), ())), preferred_element_type=f32)


def dot_tn(a, b):
    return lax.dot_general(a, b, (((0,), (0,)), ((), ())), preferred_element_type=f32)


def rope_tables(length):
    frequency = rope_base ** (-np.arange(0, HEAD_DIM, 2, dtype=np.float32) / HEAD_DIM)
    blocks = np.arange(length).reshape(-1, 2, HEAD_DIM)
    orders = np.stack([blocks.reshape(-1), blocks[:, ::-1].reshape(-1)])
    angles = orders.astype(np.float32)[:, :, None] * frequency.astype(np.float32)
    cos = np.tile(np.cos(angles), (1, 1, 4)).astype(np.float32)
    sin = np.sin(angles).astype(np.float32)
    sin = np.concatenate([-sin, sin, -sin, sin], axis=-1)
    return cos, sin


def swap_halves(values):
    lane = lax.broadcasted_iota(jnp.int32, values.shape, 1)
    low = lax.rem(lane, HEAD_DIM) < HEAD_DIM // 2
    return jnp.where(low, pltpu.roll(values, WIDE - 32, 1), pltpu.roll(values, 32, 1))


def head_only(values, head):
    lane = lax.broadcasted_iota(jnp.int32, values.shape, 1)
    inside = (lane < HEAD_DIM) if head == 0 else (lane >= HEAD_DIM)
    return jnp.where(inside, values, jnp.zeros_like(values))


def join_heads(first, second):
    lane = lax.broadcasted_iota(jnp.int32, first.shape, 1)
    return jnp.where(lane < HEAD_DIM, first, second)


def attend_kernel(visit, first, w_qkv, w_out, cos, sin, part, q, k, v, att, lse):
    tokens = first.shape[0]

    @pl.loop(0, tokens // BLOCK)
    def _(i):
        rows = pl.ds(pl.multiple_of(i * BLOCK, BLOCK), BLOCK)
        packed = dot_nn(first[rows, :], w_qkv[...])
        c, s = cos[rows, :], sin[rows, :]
        pq, pk = packed[:, :WIDE], packed[:, WIDE : 2 * WIDE]
        q[rows, :] = (pq * c + swap_halves(pq) * s).astype(bf16)
        k[rows, :] = (pk * c + swap_halves(pk) * s).astype(bf16)
        v[rows, :] = packed[:, 2 * WIDE :].astype(bf16)

    size = tokens // len(visit)
    for i, sent in visit:
        rows = pl.ds(pl.multiple_of(i * size, size), size)
        q_rows = q[rows, :]
        outs = []
        for head in range(2):
            scores = dot_nt(head_only(q_rows, head), k[...]) * HEAD_DIM**-0.5
            top = jnp.max(scores, axis=-1, keepdims=True)
            exponent = jnp.exp(scores - top)
            total = jnp.sum(exponent, axis=-1, keepdims=True)
            weights = (exponent * (1.0 / total)).astype(bf16)
            outs.append(dot_nn(weights, v[...]))
            lse[rows, head : head + 1] = top + jnp.log(total)
        joined = join_heads(*outs).astype(bf16)
        att[rows, :] = joined
        part[rows, :] = dot_nn(joined, w_out[...]).astype(bf16)
        sent.start()


def attend_back_kernel(
    visit, between, branch, first, w_qkv, w_out, cos, sin, q, k, v, att, lse,
    part, grad_qkv, grad_out, dpacked, dk, dv,
):
    tokens = branch.shape[0]
    dk[...] = jnp.zeros_like(dk)
    dv[...] = jnp.zeros_like(dv)

    @pl.loop(0, tokens // BLOCK)
    def _(i):
        rows = pl.ds(pl.multiple_of(i * BLOCK, BLOCK), BLOCK)
        grad = dot_nt(branch[rows, :], w_out[...]).astype(bf16)
        q_rows = q[rows, :]
        dqs, dks, dvs = [], [], []
        for head in range(2):
            scores = dot_nt(head_only(q_rows, head), k[...]) * HEAD_DIM**-0.5
            probs = jnp.exp(scores - lse[rows, head : head + 1])
            dvs.append(dot_tn(probs.astype(bf16), grad))
            dprobs = dot_nt(head_only(grad, head), v[...])
            dot_sum = jnp.sum(probs * dprobs, axis=-1, keepdims=True)
            dscores = (probs * (dprobs - dot_sum)).astype(bf16)
            dqs.append(dot_nn(dscores, k[...]))
            dks.append(dot_tn(dscores, q_rows))
        dk[...] += join_heads(*dks)
        dv[...] += join_heads(*dvs)
        dq = join_heads(*dqs) * HEAD_DIM**-0.5
        dq = dq * cos[rows, :] - swap_halves(dq) * sin[rows, :]
        dpacked[rows, :WIDE] = dq.astype(bf16)

    between()
    size = tokens // len(visit)
    for i, sent in visit:
        rows = pl.ds(pl.multiple_of(i * size, size), size)
        d = dk[rows, :] * HEAD_DIM**-0.5
        d = d * cos[rows, :] - swap_halves(d) * sin[rows, :]
        dpacked[rows, WIDE : 2 * WIDE] = d.astype(bf16)
        dpacked[rows, 2 * WIDE :] = dv[rows, :].astype(bf16)
        part[rows, :] = dot_nt(dpacked[rows, :], w_qkv[...]).astype(bf16)
        sent.start()

    grad_out[...] = dot_tn(att[...], branch[...]).astype(bf16)

    @pl.loop(0, first.shape[1] // BLOCK)
    def _(i):
        cols = pl.ds(pl.multiple_of(i * BLOCK, BLOCK), BLOCK)
        grad_qkv[cols, :] = dot_tn(first[:, cols], dpacked[...]).astype(bf16)


def call(kernel, ident, outs, scratch, *args):
    vmem = pl.BlockSpec(memory_space=pltpu.VMEM)
    return pl.pallas_call(
        kernel,
        out_shape=[jax.ShapeDtypeStruct(s, d) for s, d in outs],
        in_specs=[vmem] * len(args),
        out_specs=[vmem] * len(outs),
        scratch_shapes=[pltpu.VMEM(*x) if isinstance(x, tuple) else x for x in scratch],
        compiler_params=pltpu.CompilerParams(
            collective_id=ident, has_side_effects=True, vmem_limit_bytes=48 * 2**20
        ),
    )(*args)


def visits(far, across, shards):
    return [(far(d), across[d]) for d in list(range(1, shards)) + [0]]


def attend_send_kernel(
    shards, first, w_qkv, w_out, cos, sin, ffn_blocks,
    attn_sum, ffn_own, q, k, v, att, lse, part, send1, recv1, ybuf, zbuf, send2, recv2,
):
    env = greet(shards, True)
    spread = spread_moves(ffn_blocks, ffn_own, send2, recv2, [], shards, *env)
    scatter = scatter_moves(part, attn_sum, send1, recv1, [ybuf, zbuf], shards, *env)
    spread[0]()
    attend_kernel(
        visits(env[3], scatter[3], shards),
        first, w_qkv, w_out, cos, sin, part, q, k, v, att, lse,
    )
    scatter[1]()
    spread[1]()
    scatter[2]()
    spread[2]()


def attend_back_send_kernel(
    shards, branch, first, w_qkv, w_out, cos, sin, q, k, v, att, lse, down_part, ffn_halves,
    grad_first, down_sum, ffn_sum, grad_qkv, grad_out, part, dpacked, dk, dv,
    send1, recv1, ybuf1, zbuf1, send2, recv2, ybuf2, zbuf2, send3, recv3,
):
    env = greet(shards, False)
    scatter = scatter_moves(part, grad_first, send1, recv1, [ybuf1, zbuf1], shards, *env)
    down = scatter_moves(down_part, down_sum, send2, recv2, [ybuf2, zbuf2], shards, *env)
    swap = swap_moves(ffn_halves, ffn_sum, send3, recv3, [], shards, *env)
    down[0]()
    swap[0]()
    attend_back_kernel(
        visits(env[3], scatter[3], shards), down[1],
        branch, first, w_qkv, w_out, cos, sin, q, k, v, att, lse,
        part, grad_qkv, grad_out, dpacked, dk, dv,
    )
    scatter[1]()
    down[2]()
    swap[1]()
    scatter[2]()
    swap[2]()


def sems(count):
    return [pltpu.SemaphoreType.DMA((count,))] * 2


def scatter_scratch(shards, rows, features):
    return sems(2 * shards) + [
        ((2 * shards, rows, features), bf16), ((shards, rows, features), bf16)
    ]


def greet(shards, spreads):
    s, y, c = (lax.axis_index(name) for name in ("shard", "cy", "core"))
    chips = 2 * shards
    me = 2 * s + y
    barrier = pltpu.get_barrier_semaphore()
    for step in range(1, chips):
        peer = lax.rem(me + step, chips)
        pl.semaphore_signal(
            barrier, inc=1, device_id=at_chip(peer // 2, lax.rem(peer, 2)), device_id_type=MESH
        )
    if spreads:
        pl.semaphore_signal(barrier, inc=1, device_id={"core": 1 - c}, device_id_type=MESH)
    pl.semaphore_wait(barrier, chips if spreads else chips - 1)

    def far(d):
        return lax.rem(s + d, shards)

    return s, y, c, far


def comm_kernel(shards, kinds, *refs):
    count = len(kinds)
    ins, outs, rest = refs[:count], refs[count : 2 * count], list(refs[2 * count :])
    env = greet(shards, "spread" in kinds)
    stages = [[], [], []]
    for kind, src, dst in zip(kinds, ins, outs):
        send, recv = rest.pop(0), rest.pop(0)
        scratch = [rest.pop(0) for _ in range(2 if kind == "rs" else 0)]
        for stage, step in zip(stages, MOVES[kind](src, dst, send, recv, scratch, shards, *env)):
            stage.append(step)
    for stage in stages:
        for step in stage:
            step()


MESH = pl.DeviceIdType.MESH


def at_chip(shard, cy):
    return {"shard": shard, "cy": cy}


def remote(src, dst, send, recv, where):
    return pltpu.make_async_remote_copy(
        src_ref=src, dst_ref=dst, send_sem=send, recv_sem=recv, device_id=where, device_id_type=MESH
    )


def gather_moves(src, dst, send, recv, scratch, shards, s, y, c, far):
    size = src.shape[0]
    cuts = 4 if size % 64 == 0 else 1
    step = size // cuts

    def place(shard, cy, cut=0, rows=size):
        start = pl.multiple_of((2 * shard + cy) * size + cut * step, step)
        return dst.at[pl.ds(start, rows), :]

    across = remote(src, place(s, y), send.at[0], recv.at[0], at_chip(s, 1 - y))
    along, onward = [], []
    for cut in range(cuts):
        for d in range(1, shards):
            slot = 1 + cut * 2 * shards + d
            along.append(
                remote(
                    src.at[pl.ds(cut * step, step), :], place(s, y, cut, step),
                    send.at[slot], recv.at[slot], at_chip(far(d), y),
                )
            )
            spot = place(far(shards - d), y, cut, step)
            slot += shards
            onward.append(remote(spot, spot, send.at[slot], recv.at[slot], at_chip(s, 1 - y)))

    def begin():
        for copy in along[: shards - 1]:
            copy.start()
        across.start()
        for copy in along[shards - 1 :]:
            copy.start()
        place(s, y)[...] = src[...]

    def middle():
        for first, second in zip(along, onward):
            first.wait_recv()
            second.start()

    def finish():
        for copy in along:
            copy.wait_send()
        across.wait()
        for copy in onward:
            copy.wait()

    return begin, middle, finish


def scatter_moves(src, dst, send, recv, scratch, shards, s, y, c, far):
    size = dst.shape[0]
    ybuf, zbuf = scratch

    def part(shard, cy):
        return src.at[pl.ds(pl.multiple_of((2 * shard + cy) * size, size), size), :]

    order = list(range(1, shards)) + [0]
    across = {
        d: remote(part(far(d), 1 - y), ybuf.at[d], send.at[d], recv.at[d], at_chip(s, 1 - y))
        for d in order
    }
    along = {
        d: remote(
            ybuf.at[shards + d], zbuf.at[d], send.at[shards + d], recv.at[shards + d],
            at_chip(far(d), y),
        )
        for d in range(1, shards)
    }

    def begin():
        for d in order:
            across[d].start()

    def middle():
        for d in range(1, shards):
            across[d].wait_recv()
            ybuf[shards + d] = (part(far(d), y)[...].astype(f32) + ybuf[d].astype(f32)).astype(bf16)
            along[d].start()

    def finish():
        across[0].wait_recv()
        total = part(s, y)[...].astype(f32) + ybuf[0].astype(f32)
        for d in range(1, shards):
            along[d].wait_recv()
            total = total + zbuf[d].astype(f32)
        dst[...] = total
        for d in order:
            across[d].wait_send()
        for d in range(1, shards):
            along[d].wait_send()

    return begin, middle, finish, across


def swap_moves(src, dst, send, recv, scratch, shards, s, y, c, far, share=False):
    chips, size = 2 * shards, src.shape[1]
    me = 2 * s + y

    def place(chip):
        if share:
            return dst.at[chip, pl.ds(pl.multiple_of(c * size, size), size), :]
        return dst.at[chip]

    out, onward = [], []
    for e in range(1, chips):
        peer = lax.rem(me + e, chips)
        out.append(
            remote(
                src.at[peer], place(me), send.at[e], recv.at[e],
                at_chip(peer // 2, lax.rem(peer, 2)),
            )
        )
    for e in range(chips if share else 0):
        spot = place(lax.rem(me + chips - e, chips))
        first = src.at[me] if e == 0 else spot
        onward.append(remote(first, spot, send.at[chips + e], recv.at[chips + e], {"core": 1 - c}))

    def begin():
        for copy in out:
            copy.start()
        if share:
            onward[0].start()
        place(me)[...] = src[me]

    def middle():
        for e in range(1, chips):
            out[e - 1].wait_recv()
            if share:
                onward[e].start()

    def finish():
        for copy in out:
            copy.wait_send()
        for copy in onward:
            copy.wait()

    return begin, middle, finish


def spread_moves(*args):
    return swap_moves(*args, share=True)


MOVES = {"ag": gather_moves, "rs": scatter_moves, "a2a": swap_moves, "spread": spread_moves}


def exchange(shards, ident, *jobs):
    chips = 2 * shards
    outs, scratch = [], []
    for kind, value in jobs:
        shape, dtype = value.shape, value.dtype
        slots = {"ag": 4 * chips + 1, "rs": chips, "a2a": chips, "spread": 2 * chips}[kind]
        scratch += [pltpu.SemaphoreType.DMA((slots,))] * 2
        if kind == "ag":
            shape = (chips * shape[0], shape[1])
        elif kind == "rs":
            shape, dtype = (shape[0] // chips, shape[1]), f32
            scratch += [pltpu.VMEM((chips,) + shape, bf16), pltpu.VMEM((shards,) + shape, bf16)]
        elif kind == "spread":
            shape = (shape[0], 2 * shape[1], shape[2])
        outs.append(jax.ShapeDtypeStruct(shape, dtype))
    vmem = pl.BlockSpec(memory_space=pltpu.VMEM)
    kinds = tuple(kind for kind, _ in jobs)
    return pl.pallas_call(
        lambda *refs: comm_kernel(shards, kinds, *refs),
        out_shape=outs,
        in_specs=[vmem] * len(jobs),
        out_specs=[vmem] * len(jobs),
        scratch_shapes=scratch,
        compiler_params=pltpu.CompilerParams(
            collective_id=ident, has_side_effects=True, vmem_limit_bytes=48 * 2**20
        ),
    )(*[value for _, value in jobs])


def gate_mix(upward):
    half_width = upward.shape[1] // 2
    return jax.nn.gelu(upward[:, :half_width], approximate=False) * upward[:, half_width:]


def swap_core(value):
    return lax.ppermute(value, "core", [(0, 1), (1, 0)])


def on_device(replicas, shards, hidden, cotangent, w_qkv, w_out, w_in, w_down, norm_attn, norm_ffn):
    _, local_len, features = hidden.shape
    chips = 2 * shards
    units = w_down.shape[0] // chips
    core = lax.axis_index("core")
    take = lambda value, axis, index: lax.dynamic_index_in_dim(value, index, axis, keepdims=False)

    gain_pair = jnp.concatenate([norm_attn, norm_ffn])
    gain_other = swap_core(gain_pair)
    gain_rows = jnp.where(
        core == 0, jnp.stack([gain_pair, gain_other]), jnp.stack([gain_other, gain_pair])
    )
    (gains,) = exchange(shards, 0, ("ag", jnp.pad(gain_rows, ((0, 14), (0, 0)))))
    gains = gains.reshape(chips, 16, 2, -1)[:, :2].transpose(2, 0, 1, 3).reshape(2, features)
    gains = gains.astype(f32)
    other = swap_core(jnp.stack([take(hidden, 0, 1 - core), take(cotangent, 0, 1 - core)]))
    x = jnp.concatenate([take(hidden, 0, core), other[0]]).astype(f32)
    grad_top = jnp.concatenate([take(cotangent, 0, core), other[1]])

    rows = w_qkv.shape[0]
    qkv_blocks = (
        w_qkv.reshape(rows, 3, chips, WIDE).transpose(2, 0, 1, 3).reshape(chips, rows, 3 * WIDE)
    )
    ffn_blocks = jnp.concatenate(
        [
            w_in.reshape(rows, 2, chips, units).transpose(2, 0, 1, 3).reshape(chips, rows, -1),
            w_down.reshape(chips, units, rows).transpose(0, 2, 1),
        ],
        axis=2,
    )
    out_own = lax.all_gather(w_out, "core", axis=0, tiled=True)

    def gather(value):
        return lax.all_gather(value, CHIPS, axis=0, tiled=True)

    normed_one, centered_one, inverse_one = layer_norm(x, gains[0])
    first, qkv_own = exchange(
        shards, 1, ("ag", normed_one.astype(bf16)), ("spread", qkv_blocks)
    )
    qkv_own = qkv_own.reshape(features, 3 * WIDE)
    top_all = gather(grad_top)
    tokens = first.shape[0]
    cos_np, sin_np = rope_tables(tokens)
    cos = take(jnp.asarray(cos_np), 0, core)
    sin = take(jnp.asarray(sin_np), 0, core)
    narrow = ((tokens, WIDE), bf16)
    own_rows = x.shape[0]
    attn_sum, ffn_own, q, k, v, att, lse = call(
        lambda *refs: attend_send_kernel(shards, *refs),
        2,
        [
            ((own_rows, features), f32), ((chips, 2 * rows, 3 * units), bf16),
            narrow, narrow, narrow, narrow, ((tokens, 2), f32),
        ],
        [((tokens, features), bf16)]
        + scatter_scratch(shards, own_rows, features)
        + sems(2 * chips),
        first, qkv_own, out_own, cos, sin, ffn_blocks,
    )
    ffn_own = ffn_own.reshape(features, 3 * units)
    in_own, down_own = ffn_own[:, : 2 * units], ffn_own[:, 2 * units :]
    residual = x + attn_sum
    normed_two, centered_two, inverse_two = layer_norm(residual, gains[1])
    (second,) = exchange(shards, 3, ("ag", normed_two.astype(bf16)))
    upward = dot_nn(second, in_own)
    gated, gate_back = jax.vjp(gate_mix, upward)
    gated = gated.astype(bf16)
    grad_gated = dot_nn(top_all, down_own)
    grad_up = gate_back(grad_gated)[0].astype(bf16)
    down_part = dot_nt(gated, down_own).astype(bf16)
    (grad_second,) = exchange(shards, 4, ("rs", dot_nt(grad_up, in_own).astype(bf16)))
    grad_norm_two, grad_gain_ffn = norm_back(grad_second, centered_two, inverse_two, gains[1])
    grad_resid = grad_top.astype(f32) + grad_norm_two
    (branch,) = exchange(shards, 5, ("ag", grad_resid.astype(bf16)))
    grad_ffn = jnp.concatenate(
        [dot_tn(second, grad_up).astype(bf16), dot_tn(top_all, gated).astype(bf16)], axis=1
    )

    def over_core(value):
        return take(value, 1, core).astype(f32) + swap_core(take(value, 1, 1 - core)).astype(f32)

    def over_replicas(value):
        if replicas == 2:
            return value.astype(f32) + lax.ppermute(value, "replica", [(0, 1), (1, 0)]).astype(f32)
        return lax.psum(value, "replica").astype(f32)

    def halves(value):
        return over_core(value.reshape(chips, 2, rows, value.shape[-1])).astype(bf16)

    grad_first, down_sum, ffn_sum, grad_qkv, grad_out = call(
        lambda *refs: attend_back_send_kernel(shards, *refs),
        6,
        [
            ((own_rows, features), f32), ((own_rows, features), f32),
            ((chips, rows, 3 * units), bf16),
            ((features, 3 * WIDE), bf16), ((WIDE, features), bf16),
        ],
        [
            ((tokens, features), bf16), ((tokens, 3 * WIDE), bf16),
            ((tokens, WIDE), f32), ((tokens, WIDE), f32),
        ]
        + scatter_scratch(shards, own_rows, features) * 2
        + sems(chips),
        branch, first, qkv_own, out_own, cos, sin, q, k, v, att, lse,
        down_part, halves(grad_ffn),
    )
    block_out = (residual + down_sum).astype(bf16)
    ffn_sum = over_replicas(ffn_sum)
    grad_in = ffn_sum[:, :, : 2 * units].reshape(chips, rows, 2, units)
    grad_in = grad_in.transpose(1, 2, 0, 3).reshape(w_in.shape)
    grad_down = ffn_sum[:, :, 2 * units :].transpose(0, 2, 1).reshape(w_down.shape)
    grad_norm_one, grad_gain_attn = norm_back(grad_first, centered_one, inverse_one, gains[0])
    grad_hidden = (grad_resid + grad_norm_one).astype(bf16)
    grad_out = over_core(grad_out.reshape(1, 2, rows, features))[0].astype(bf16)
    grad_out = over_replicas(grad_out)

    gain_parts = jnp.stack([grad_gain_attn, grad_gain_ffn])
    gain_parts = gain_parts.reshape(2, chips, 2, rows)
    gain_half = take(gain_parts, 2, core) + swap_core(take(gain_parts, 2, 1 - core))
    gain_half = gain_half.transpose(1, 0, 2).reshape(chips, 1, 2 * rows)
    qkv_sum, gain_sum = exchange(
        shards, 7, ("a2a", halves(grad_qkv)), ("a2a", jnp.broadcast_to(gain_half, (chips, 8, 2 * rows)))
    )
    gain_sum = over_replicas(jnp.sum(gain_sum[:, 0], axis=0)).reshape(2, rows)

    qkv_sum = over_replicas(qkv_sum)
    grad_qkv = qkv_sum.reshape(chips, rows, 3, WIDE).transpose(1, 2, 0, 3).reshape(w_qkv.shape)
    done = jnp.stack([block_out, grad_hidden])
    back = swap_core(done[:, local_len:])
    mine = done[:, :local_len]
    pair = jnp.where(core == 0, jnp.stack([mine, back], 1), jnp.stack([back, mine], 1))
    return (pair[0], pair[1], grad_qkv, grad_out, grad_in, grad_down, gain_sum[0], gain_sum[1])


def solution(mesh):
    replicas, shards, ctx = (mesh.shape[name] for name in ("replica", "shard", "ctx"))
    fine = Mesh(
        mesh.devices.reshape(replicas, shards, ctx // 2, 2), ("replica", "shard", "cy", "core")
    )
    group = ("shard", "cy", "core")
    token = P("replica", group, None)
    row, col, vec = P(group, None), P(None, group), P(group)

    def body(*args):
        return on_device(replicas, shards, *args)

    return jax.shard_map(
        body,
        mesh=fine,
        in_specs=(token, token, row, row, row, col, vec, vec),
        out_specs=(token, token, row, row, row, col, vec, vec),
        check_vma=False,
    )
```

```python
import jax
import jax.numpy as jnp
import numpy as np
from jax import lax
from jax.experimental import pallas as pl
from jax.experimental.pallas import tpu as pltpu
from jax.sharding import Mesh, PartitionSpec as P

HEAD_DIM = 64
norm_eps = 1e-05
rope_base = 160000.0
f32 = jnp.float32
bf16 = jnp.bfloat16
CHIPS = ("shard", "cy")
WIDE = 128
BLOCK = 256


def layer_norm(values, scale_row):
    center = values - jnp.mean(values, axis=-1, keepdims=True)
    inverse = lax.rsqrt(jnp.mean(center * center, axis=-1, keepdims=True) + norm_eps)
    normed = center * inverse
    return (normed * scale_row, normed, inverse)


def norm_back(grad_norm, normed, inverse, scale_row):
    scaled = grad_norm * scale_row
    grad_gain = jnp.sum(grad_norm * normed, axis=0)
    grad_input = inverse * (
        scaled
        - jnp.mean(scaled, axis=-1, keepdims=True)
        - normed * jnp.mean(scaled * normed, axis=-1, keepdims=True)
    )
    return (grad_input, grad_gain)


def dot_nn(a, b):
    return lax.dot_general(a, b, (((1,), (0,)), ((), ())), preferred_element_type=f32)


def dot_nt(a, b):
    return lax.dot_general(a, b, (((1,), (1,)), ((), ())), preferred_element_type=f32)


def dot_tn(a, b):
    return lax.dot_general(a, b, (((0,), (0,)), ((), ())), preferred_element_type=f32)


def rope_tables(length):
    frequency = rope_base ** (-np.arange(0, HEAD_DIM, 2, dtype=np.float32) / HEAD_DIM)
    blocks = np.arange(length).reshape(-1, 2, HEAD_DIM)
    orders = np.stack([blocks.reshape(-1), blocks[:, ::-1].reshape(-1)])
    angles = orders.astype(np.float32)[:, :, None] * frequency.astype(np.float32)
    cos = np.tile(np.cos(angles), (1, 1, 4)).astype(np.float32)
    sin = np.sin(angles).astype(np.float32)
    sin = np.concatenate([-sin, sin, -sin, sin], axis=-1)
    return cos, sin


def swap_halves(values):
    lane = lax.broadcasted_iota(jnp.int32, values.shape, 1)
    low = lax.rem(lane, HEAD_DIM) < HEAD_DIM // 2
    return jnp.where(low, pltpu.roll(values, WIDE - 32, 1), pltpu.roll(values, 32, 1))


def head_only(values, head):
    lane = lax.broadcasted_iota(jnp.int32, values.shape, 1)
    inside = (lane < HEAD_DIM) if head == 0 else (lane >= HEAD_DIM)
    return jnp.where(inside, values, jnp.zeros_like(values))


def join_heads(first, second):
    lane = lax.broadcasted_iota(jnp.int32, first.shape, 1)
    return jnp.where(lane < HEAD_DIM, first, second)


def attend_kernel(visit, first, w_qkv, w_out, cos, sin, part, q, k, v, att, lse):
    tokens = first.shape[0]

    @pl.loop(0, tokens // BLOCK)
    def _(i):
        rows = pl.ds(pl.multiple_of(i * BLOCK, BLOCK), BLOCK)
        packed = dot_nn(first[rows, :], w_qkv[...])
        c, s = cos[rows, :], sin[rows, :]
        pq, pk = packed[:, :WIDE], packed[:, WIDE : 2 * WIDE]
        q[rows, :] = (pq * c + swap_halves(pq) * s).astype(bf16)
        k[rows, :] = (pk * c + swap_halves(pk) * s).astype(bf16)
        v[rows, :] = packed[:, 2 * WIDE :].astype(bf16)

    size = tokens // len(visit)
    for i, sent in visit:
        rows = pl.ds(pl.multiple_of(i * size, size), size)
        q_rows = q[rows, :]
        outs = []
        for head in range(2):
            scores = dot_nt(head_only(q_rows, head), k[...]) * HEAD_DIM**-0.5
            top = jnp.max(scores, axis=-1, keepdims=True)
            exponent = jnp.exp(scores - top)
            total = jnp.sum(exponent, axis=-1, keepdims=True)
            weights = (exponent * (1.0 / total)).astype(bf16)
            outs.append(dot_nn(weights, v[...]))
            lse[rows, head : head + 1] = top + jnp.log(total)
        joined = join_heads(*outs).astype(bf16)
        att[rows, :] = joined
        part[rows, :] = dot_nn(joined, w_out[...]).astype(bf16)
        sent.start()


def attend_back_kernel(
    visit, between, branch, first, w_qkv, w_out, cos, sin, q, k, v, att, lse,
    part, grad_qkv, grad_out, dpacked, dk, dv,
):
    tokens = branch.shape[0]
    dk[...] = jnp.zeros_like(dk)
    dv[...] = jnp.zeros_like(dv)

    @pl.loop(0, tokens // BLOCK)
    def _(i):
        rows = pl.ds(pl.multiple_of(i * BLOCK, BLOCK), BLOCK)
        grad = dot_nt(branch[rows, :], w_out[...]).astype(bf16)
        q_rows = q[rows, :]
        dqs, dks, dvs = [], [], []
        for head in range(2):
            scores = dot_nt(head_only(q_rows, head), k[...]) * HEAD_DIM**-0.5
            probs = jnp.exp(scores - lse[rows, head : head + 1])
            dvs.append(dot_tn(probs.astype(bf16), grad))
            dprobs = dot_nt(head_only(grad, head), v[...])
            dot_sum = jnp.sum(probs * dprobs, axis=-1, keepdims=True)
            dscores = (probs * (dprobs - dot_sum)).astype(bf16)
            dqs.append(dot_nn(dscores, k[...]))
            dks.append(dot_tn(dscores, q_rows))
        dk[...] += join_heads(*dks)
        dv[...] += join_heads(*dvs)
        dq = join_heads(*dqs) * HEAD_DIM**-0.5
        dq = dq * cos[rows, :] - swap_halves(dq) * sin[rows, :]
        dpacked[rows, :WIDE] = dq.astype(bf16)

    between()
    size = tokens // len(visit)
    for i, sent in visit:
        rows = pl.ds(pl.multiple_of(i * size, size), size)
        d = dk[rows, :] * HEAD_DIM**-0.5
        d = d * cos[rows, :] - swap_halves(d) * sin[rows, :]
        dpacked[rows, WIDE : 2 * WIDE] = d.astype(bf16)
        dpacked[rows, 2 * WIDE :] = dv[rows, :].astype(bf16)
        part[rows, :] = dot_nt(dpacked[rows, :], w_qkv[...]).astype(bf16)
        sent.start()

    grad_out[...] = dot_tn(att[...], branch[...]).astype(bf16)

    @pl.loop(0, first.shape[1] // BLOCK)
    def _(i):
        cols = pl.ds(pl.multiple_of(i * BLOCK, BLOCK), BLOCK)
        grad_qkv[cols, :] = dot_tn(first[:, cols], dpacked[...]).astype(bf16)


def call(kernel, ident, outs, scratch, *args):
    vmem = pl.BlockSpec(memory_space=pltpu.VMEM)
    return pl.pallas_call(
        kernel,
        out_shape=[jax.ShapeDtypeStruct(s, d) for s, d in outs],
        in_specs=[vmem] * len(args),
        out_specs=[vmem] * len(outs),
        scratch_shapes=[pltpu.VMEM(*x) if isinstance(x, tuple) else x for x in scratch],
        compiler_params=pltpu.CompilerParams(
            collective_id=ident, has_side_effects=True, vmem_limit_bytes=48 * 2**20
        ),
    )(*args)


def visits(far, across, shards):
    return [(far(d), across[d]) for d in list(range(1, shards)) + [0]]


def attend_send_kernel(
    shards, first, w_qkv, w_out, cos, sin, ffn_blocks, top,
    attn_sum, ffn_own, top_all, q, k, v, att, lse, part, send1, recv1, ybuf, zbuf, send2, recv2,
    send3, recv3,
):
    env = greet(shards, True)
    spread = spread_moves(ffn_blocks, ffn_own, send2, recv2, [], shards, *env)
    scatter = scatter_moves(part, attn_sum, send1, recv1, [ybuf, zbuf], shards, *env)
    tops = gather_moves(top, top_all, send3, recv3, [], shards, *env)
    tops[0]()
    spread[0]()
    attend_kernel(
        visits(env[3], scatter[3], shards),
        first, w_qkv, w_out, cos, sin, part, q, k, v, att, lse,
    )
    tops[1]()
    scatter[1]()
    spread[1]()
    scatter[2]()
    spread[2]()
    tops[2]()


def attend_back_send_kernel(
    shards, branch, first, w_qkv, w_out, cos, sin, q, k, v, att, lse, down_part, ffn_halves,
    grad_first, down_sum, ffn_sum, grad_qkv, grad_out, part, dpacked, dk, dv,
    send1, recv1, ybuf1, zbuf1, send2, recv2, ybuf2, zbuf2, send3, recv3,
):
    env = greet(shards, False)
    scatter = scatter_moves(part, grad_first, send1, recv1, [ybuf1, zbuf1], shards, *env)
    down = scatter_moves(down_part, down_sum, send2, recv2, [ybuf2, zbuf2], shards, *env)
    swap = swap_moves(ffn_halves, ffn_sum, send3, recv3, [], shards, *env)
    down[0]()
    swap[0]()
    attend_back_kernel(
        visits(env[3], scatter[3], shards), down[1],
        branch, first, w_qkv, w_out, cos, sin, q, k, v, att, lse,
        part, grad_qkv, grad_out, dpacked, dk, dv,
    )
    scatter[1]()
    down[2]()
    swap[1]()
    scatter[2]()
    swap[2]()


def sems(count):
    return [pltpu.SemaphoreType.DMA((count,))] * 2


def scatter_scratch(shards, rows, features):
    return sems(2 * shards) + [
        ((2 * shards, rows, features), bf16), ((shards, rows, features), bf16)
    ]


def greet(shards, spreads):
    s, y, c = (lax.axis_index(name) for name in ("shard", "cy", "core"))
    chips = 2 * shards
    me = 2 * s + y
    barrier = pltpu.get_barrier_semaphore()
    for step in range(1, chips):
        peer = lax.rem(me + step, chips)
        pl.semaphore_signal(
            barrier, inc=1, device_id=at_chip(peer // 2, lax.rem(peer, 2)), device_id_type=MESH
        )
    if spreads:
        pl.semaphore_signal(barrier, inc=1, device_id={"core": 1 - c}, device_id_type=MESH)
    pl.semaphore_wait(barrier, chips if spreads else chips - 1)

    def far(d):
        return lax.rem(s + d, shards)

    return s, y, c, far


def comm_kernel(shards, kinds, *refs):
    count = len(kinds)
    ins, outs, rest = refs[:count], refs[count : 2 * count], list(refs[2 * count :])
    env = greet(shards, "spread" in kinds)
    stages = [[], [], []]
    for kind, src, dst in zip(kinds, ins, outs):
        send, recv = rest.pop(0), rest.pop(0)
        scratch = [rest.pop(0) for _ in range(2 if kind == "rs" else 0)]
        for stage, step in zip(stages, MOVES[kind](src, dst, send, recv, scratch, shards, *env)):
            stage.append(step)
    for stage in stages:
        for step in stage:
            step()


MESH = pl.DeviceIdType.MESH


def at_chip(shard, cy):
    return {"shard": shard, "cy": cy}


def remote(src, dst, send, recv, where):
    return pltpu.make_async_remote_copy(
        src_ref=src, dst_ref=dst, send_sem=send, recv_sem=recv, device_id=where, device_id_type=MESH
    )


def gather_moves(src, dst, send, recv, scratch, shards, s, y, c, far):
    size = src.shape[0]
    cuts = 4 if size % 64 == 0 else 1
    step = size // cuts

    def place(shard, cy, cut=0, rows=size):
        start = pl.multiple_of((2 * shard + cy) * size + cut * step, step)
        return dst.at[pl.ds(start, rows), :]

    across = remote(src, place(s, y), send.at[0], recv.at[0], at_chip(s, 1 - y))
    along, onward = [], []
    for cut in range(cuts):
        for d in range(1, shards):
            slot = 1 + cut * 2 * shards + d
            along.append(
                remote(
                    src.at[pl.ds(cut * step, step), :], place(s, y, cut, step),
                    send.at[slot], recv.at[slot], at_chip(far(d), y),
                )
            )
            spot = place(far(shards - d), y, cut, step)
            slot += shards
            onward.append(remote(spot, spot, send.at[slot], recv.at[slot], at_chip(s, 1 - y)))

    def begin():
        for copy in along[: shards - 1]:
            copy.start()
        across.start()
        for copy in along[shards - 1 :]:
            copy.start()
        place(s, y)[...] = src[...]

    def middle():
        for first, second in zip(along, onward):
            first.wait_recv()
            second.start()

    def finish():
        for copy in along:
            copy.wait_send()
        across.wait()
        for copy in onward:
            copy.wait()

    return begin, middle, finish


def scatter_moves(src, dst, send, recv, scratch, shards, s, y, c, far):
    size = dst.shape[0]
    ybuf, zbuf = scratch

    def part(shard, cy):
        return src.at[pl.ds(pl.multiple_of((2 * shard + cy) * size, size), size), :]

    order = list(range(1, shards)) + [0]
    across = {
        d: remote(part(far(d), 1 - y), ybuf.at[d], send.at[d], recv.at[d], at_chip(s, 1 - y))
        for d in order
    }
    along = {
        d: remote(
            ybuf.at[shards + d], zbuf.at[d], send.at[shards + d], recv.at[shards + d],
            at_chip(far(d), y),
        )
        for d in range(1, shards)
    }

    def begin():
        for d in order:
            across[d].start()

    def middle():
        for d in range(1, shards):
            across[d].wait_recv()
            ybuf[shards + d] = (part(far(d), y)[...].astype(f32) + ybuf[d].astype(f32)).astype(bf16)
            along[d].start()

    def finish():
        across[0].wait_recv()
        total = part(s, y)[...].astype(f32) + ybuf[0].astype(f32)
        for d in range(1, shards):
            along[d].wait_recv()
            total = total + zbuf[d].astype(f32)
        dst[...] = total
        for d in order:
            across[d].wait_send()
        for d in range(1, shards):
            along[d].wait_send()

    return begin, middle, finish, across


def swap_moves(src, dst, send, recv, scratch, shards, s, y, c, far, share=False):
    chips, size = 2 * shards, src.shape[1]
    me = 2 * s + y

    def place(chip):
        if share:
            return dst.at[chip, pl.ds(pl.multiple_of(c * size, size), size), :]
        return dst.at[chip]

    out, onward = [], []
    for e in range(1, chips):
        peer = lax.rem(me + e, chips)
        out.append(
            remote(
                src.at[peer], place(me), send.at[e], recv.at[e],
                at_chip(peer // 2, lax.rem(peer, 2)),
            )
        )
    for e in range(chips if share else 0):
        spot = place(lax.rem(me + chips - e, chips))
        first = src.at[me] if e == 0 else spot
        onward.append(remote(first, spot, send.at[chips + e], recv.at[chips + e], {"core": 1 - c}))

    def begin():
        for copy in out:
            copy.start()
        if share:
            onward[0].start()
        place(me)[...] = src[me]

    def middle():
        for e in range(1, chips):
            out[e - 1].wait_recv()
            if share:
                onward[e].start()

    def finish():
        for copy in out:
            copy.wait_send()
        for copy in onward:
            copy.wait()

    return begin, middle, finish


def spread_moves(*args):
    return swap_moves(*args, share=True)


MOVES = {"ag": gather_moves, "rs": scatter_moves, "a2a": swap_moves, "spread": spread_moves}


def exchange(shards, ident, *jobs):
    chips = 2 * shards
    outs, scratch = [], []
    for kind, value in jobs:
        shape, dtype = value.shape, value.dtype
        slots = {"ag": 4 * chips + 1, "rs": chips, "a2a": chips, "spread": 2 * chips}[kind]
        scratch += [pltpu.SemaphoreType.DMA((slots,))] * 2
        if kind == "ag":
            shape = (chips * shape[0], shape[1])
        elif kind == "rs":
            shape, dtype = (shape[0] // chips, shape[1]), f32
            scratch += [pltpu.VMEM((chips,) + shape, bf16), pltpu.VMEM((shards,) + shape, bf16)]
        elif kind == "spread":
            shape = (shape[0], 2 * shape[1], shape[2])
        outs.append(jax.ShapeDtypeStruct(shape, dtype))
    vmem = pl.BlockSpec(memory_space=pltpu.VMEM)
    kinds = tuple(kind for kind, _ in jobs)
    return pl.pallas_call(
        lambda *refs: comm_kernel(shards, kinds, *refs),
        out_shape=outs,
        in_specs=[vmem] * len(jobs),
        out_specs=[vmem] * len(jobs),
        scratch_shapes=scratch,
        compiler_params=pltpu.CompilerParams(
            collective_id=ident, has_side_effects=True, vmem_limit_bytes=48 * 2**20
        ),
    )(*[value for _, value in jobs])


def gate_mix(upward):
    half_width = upward.shape[1] // 2
    return jax.nn.gelu(upward[:, :half_width], approximate=False) * upward[:, half_width:]


def swap_core(value):
    return lax.ppermute(value, "core", [(0, 1), (1, 0)])


def on_device(replicas, shards, hidden, cotangent, w_qkv, w_out, w_in, w_down, norm_attn, norm_ffn):
    _, local_len, features = hidden.shape
    chips = 2 * shards
    units = w_down.shape[0] // chips
    core = lax.axis_index("core")
    take = lambda value, axis, index: lax.dynamic_index_in_dim(value, index, axis, keepdims=False)

    gain_pair = jnp.concatenate([norm_attn, norm_ffn])
    gain_other = swap_core(gain_pair)
    gain_rows = jnp.where(
        core == 0, jnp.stack([gain_pair, gain_other]), jnp.stack([gain_other, gain_pair])
    )
    (gains,) = exchange(shards, 0, ("ag", jnp.pad(gain_rows, ((0, 14), (0, 0)))))
    gains = gains.reshape(chips, 16, 2, -1)[:, :2].transpose(2, 0, 1, 3).reshape(2, features)
    gains = gains.astype(f32)
    other = swap_core(jnp.stack([take(hidden, 0, 1 - core), take(cotangent, 0, 1 - core)]))
    x = jnp.concatenate([take(hidden, 0, core), other[0]]).astype(f32)
    grad_top = jnp.concatenate([take(cotangent, 0, core), other[1]])

    rows = w_qkv.shape[0]
    qkv_blocks = (
        w_qkv.reshape(rows, 3, chips, WIDE).transpose(2, 0, 1, 3).reshape(chips, rows, 3 * WIDE)
    )
    ffn_blocks = jnp.concatenate(
        [
            w_in.reshape(rows, 2, chips, units).transpose(2, 0, 1, 3).reshape(chips, rows, -1),
            w_down.reshape(chips, units, rows).transpose(0, 2, 1),
        ],
        axis=2,
    )
    out_own = lax.all_gather(w_out, "core", axis=0, tiled=True)

    normed_one, centered_one, inverse_one = layer_norm(x, gains[0])
    first, qkv_own = exchange(
        shards, 1, ("ag", normed_one.astype(bf16)), ("spread", qkv_blocks)
    )
    qkv_own = qkv_own.reshape(features, 3 * WIDE)
    tokens = first.shape[0]
    cos_np, sin_np = rope_tables(tokens)
    cos = take(jnp.asarray(cos_np), 0, core)
    sin = take(jnp.asarray(sin_np), 0, core)
    narrow = ((tokens, WIDE), bf16)
    own_rows = x.shape[0]
    attn_sum, ffn_own, top_all, q, k, v, att, lse = call(
        lambda *refs: attend_send_kernel(shards, *refs),
        2,
        [
            ((own_rows, features), f32), ((chips, 2 * rows, 3 * units), bf16),
            ((tokens, features), bf16),
            narrow, narrow, narrow, narrow, ((tokens, 2), f32),
        ],
        [((tokens, features), bf16)]
        + scatter_scratch(shards, own_rows, features)
        + sems(2 * chips)
        + sems(4 * chips + 1),
        first, qkv_own, out_own, cos, sin, ffn_blocks, grad_top,
    )
    ffn_own = ffn_own.reshape(features, 3 * units)
    in_own, down_own = ffn_own[:, : 2 * units], ffn_own[:, 2 * units :]
    residual = x + attn_sum
    normed_two, centered_two, inverse_two = layer_norm(residual, gains[1])
    (second,) = exchange(shards, 3, ("ag", normed_two.astype(bf16)))
    upward = dot_nn(second, in_own)
    gated, gate_back = jax.vjp(gate_mix, upward)
    gated = gated.astype(bf16)
    grad_gated = dot_nn(top_all, down_own)
    grad_up = gate_back(grad_gated)[0].astype(bf16)
    down_part = dot_nt(gated, down_own).astype(bf16)
    (grad_second,) = exchange(shards, 4, ("rs", dot_nt(grad_up, in_own).astype(bf16)))
    grad_norm_two, grad_gain_ffn = norm_back(grad_second, centered_two, inverse_two, gains[1])
    grad_resid = grad_top.astype(f32) + grad_norm_two
    (branch,) = exchange(shards, 5, ("ag", grad_resid.astype(bf16)))
    grad_ffn = jnp.concatenate(
        [dot_tn(second, grad_up).astype(bf16), dot_tn(top_all, gated).astype(bf16)], axis=1
    )

    def over_core(value):
        return take(value, 1, core).astype(f32) + swap_core(take(value, 1, 1 - core)).astype(f32)

    def over_replicas(value):
        if replicas == 2:
            return value.astype(f32) + lax.ppermute(value, "replica", [(0, 1), (1, 0)]).astype(f32)
        return lax.psum(value, "replica").astype(f32)

    def halves(value):
        return over_core(value.reshape(chips, 2, rows, value.shape[-1])).astype(bf16)

    grad_first, down_sum, ffn_sum, grad_qkv, grad_out = call(
        lambda *refs: attend_back_send_kernel(shards, *refs),
        6,
        [
            ((own_rows, features), f32), ((own_rows, features), f32),
            ((chips, rows, 3 * units), bf16),
            ((features, 3 * WIDE), bf16), ((WIDE, features), bf16),
        ],
        [
            ((tokens, features), bf16), ((tokens, 3 * WIDE), bf16),
            ((tokens, WIDE), f32), ((tokens, WIDE), f32),
        ]
        + scatter_scratch(shards, own_rows, features) * 2
        + sems(chips),
        branch, first, qkv_own, out_own, cos, sin, q, k, v, att, lse,
        down_part, halves(grad_ffn),
    )
    block_out = (residual + down_sum).astype(bf16)
    ffn_sum = over_replicas(ffn_sum)
    grad_in = ffn_sum[:, :, : 2 * units].reshape(chips, rows, 2, units)
    grad_in = grad_in.transpose(1, 2, 0, 3).reshape(w_in.shape)
    grad_down = ffn_sum[:, :, 2 * units :].transpose(0, 2, 1).reshape(w_down.shape)
    grad_norm_one, grad_gain_attn = norm_back(grad_first, centered_one, inverse_one, gains[0])
    grad_hidden = (grad_resid + grad_norm_one).astype(bf16)
    grad_out = over_core(grad_out.reshape(1, 2, rows, features))[0].astype(bf16)
    grad_out = over_replicas(grad_out)

    gain_parts = jnp.stack([grad_gain_attn, grad_gain_ffn])
    gain_parts = gain_parts.reshape(2, chips, 2, rows)
    gain_half = take(gain_parts, 2, core) + swap_core(take(gain_parts, 2, 1 - core))
    gain_half = gain_half.transpose(1, 0, 2).reshape(chips, 1, 2 * rows)
    qkv_sum, gain_sum = exchange(
        shards, 7, ("a2a", halves(grad_qkv)), ("a2a", jnp.broadcast_to(gain_half, (chips, 8, 2 * rows)))
    )
    gain_sum = over_replicas(jnp.sum(gain_sum[:, 0], axis=0)).reshape(2, rows)

    qkv_sum = over_replicas(qkv_sum)
    grad_qkv = qkv_sum.reshape(chips, rows, 3, WIDE).transpose(1, 2, 0, 3).reshape(w_qkv.shape)
    done = jnp.stack([block_out, grad_hidden])
    back = swap_core(done[:, local_len:])
    mine = done[:, :local_len]
    pair = jnp.where(core == 0, jnp.stack([mine, back], 1), jnp.stack([back, mine], 1))
    return (pair[0], pair[1], grad_qkv, grad_out, grad_in, grad_down, gain_sum[0], gain_sum[1])


def solution(mesh):
    replicas, shards, ctx = (mesh.shape[name] for name in ("replica", "shard", "ctx"))
    fine = Mesh(
        mesh.devices.reshape(replicas, shards, ctx // 2, 2), ("replica", "shard", "cy", "core")
    )
    group = ("shard", "cy", "core")
    token = P("replica", group, None)
    row, col, vec = P(group, None), P(None, group), P(group)

    def body(*args):
        return on_device(replicas, shards, *args)

    return jax.shard_map(
        body,
        mesh=fine,
        in_specs=(token, token, row, row, row, col, vec, vec),
        out_specs=(token, token, row, row, row, col, vec, vec),
        check_vma=False,
    )
```
